128 devices in a mesh: field: 4 (over x), gz: 32 (over y, z, core).
Axes of the slice: x: 4, y: 4, z: 4, core: 2. Of those that a mesh axis runs over, the one named last changes fastest.
Arguments:
- fields: bfloat16 [2048, 2, 8, 16, 256], P('gz', None, 'field'), may hold values from -8 to 8
- shells: int32 [2048, 16, 256], P('gz'), may hold values from 0 to 255
- mubins: int32 [2048, 16, 256], P('gz'), may hold values from 0 to 7, as said below
Outputs:
- power: float32 [3, 8, 256], replicated
The draws below stay inside these ranges and needn't reach their ends.
Inputs may be any that keep to these rules, and one draw needn't show every extreme that they name: `mubins`: A cell's mu-bin index is never above its k-shell index.
All inputs are finite; a program needn't handle non-finite values.
Results may differ from the reference program's by a relative error of at most 0.00052.
Values may be sent and summed in bfloat16 or wider, within the bound.
No kernel may reach another device: no remote copies, remote signals or barrier semaphores. Data moves between devices by JAX's collectives and lax.ppermute only.
A program may use at most 128 MiB of HBM per device.

```python
import math
import jax
import jax.numpy as jnp
import numpy as np
from jax import lax

NZ = 2048
FIELDS = 8
SHELLS = 256
MUBINS = 8
PLANES = 16
YROWS = 256
N_FIELD = 4


def draw_fields(key, part):
    first_key, second_key, third_key = jax.random.split(jax.random.fold_in(key, 11), 3)
    common = jax.random.normal(first_key, (NZ, 2, 1, PLANES, YROWS), jnp.float32)
    mixing = jax.random.uniform(second_key, (FIELDS,), jnp.float32, 0.5, 1.0).at[0].set(1.0)
    noise = jax.random.normal(third_key, (NZ, 2, FIELDS, PLANES, YROWS), jnp.float32)
    values = mixing[None, None, :, None, None] * common + 0.7 * noise
    return jnp.clip(values, -8.0, 8.0).astype(jnp.bfloat16)


def shell_and_mu(key):
    shell_key, mu_key = jax.random.split(jax.random.fold_in(key, 23))
    shell_ids = jax.random.randint(shell_key, (NZ, PLANES, YROWS), 0, SHELLS, jnp.int32)
    upper = jnp.minimum(shell_ids + 1, MUBINS)
    mu_ids = jax.random.randint(mu_key, (NZ, PLANES, YROWS), 0, upper, jnp.int32)
    return (shell_ids, mu_ids)


def draw_shells(key, part):
    return shell_and_mu(key)[0]


def draw_mubins(key, part):
    return shell_and_mu(key)[1]


def setup_inputs(seed: int = 0) -> dict:
    seeds = jax.random.split(jax.random.key(seed), 4)
    return {
        "fields": draw_fields(jax.random.fold_in(seeds[3], 71), 0),
        "shells": draw_shells(jax.random.fold_in(seeds[3], 71), 0),
        "mubins": draw_mubins(jax.random.fold_in(seeds[3], 71), 0),
    }


def make_coef():
    table = np.zeros((3, 8, 7), np.float32)
    table[0, 0, 0] = 1.0
    table[1, 1, 0] = 1.0
    table[2, 1, 0] = -0.5
    table[2, 2, 1] = 1.5
    table[2, 3, 2] = 1.5
    table[2, 4, 3] = 1.5
    table[2, 5, 4] = 3.0
    table[2, 6, 5] = 3.0
    table[2, 7, 6] = 3.0
    return table

def dft_tables(length):
    index = jnp.arange(length, dtype=jnp.int32)
    product = index[:, None] * index[None, :] % length
    angle = product.astype(jnp.float32) * (2.0 * math.pi / length)
    factor = 1.0 / math.sqrt(length)
    return ((jnp.cos(angle) * factor).astype(jnp.bfloat16), (jnp.sin(angle) * factor).astype(jnp.bfloat16))

def monomials(wave_x, wave_y, wave_z):
    square = wave_x * wave_x + wave_y * wave_y + wave_z * wave_z
    ones = jnp.ones_like(square)
    return jnp.stack([ones, wave_x * wave_x / square, wave_y * wave_y / square, wave_z * wave_z / square, wave_x * wave_y / square, wave_x * wave_z / square, wave_y * wave_z / square])

def bin_cells(values, shell_ids, mu_ids):
    cells = values.shape[1]
    block = math.gcd(cells, 32768)
    blocks = cells // block
    value_blocks = values.reshape(3, blocks, block).transpose(1, 0, 2)
    shell_blocks = shell_ids.reshape(blocks, block)
    mu_blocks = mu_ids.reshape(blocks, block)

    def step(total, pieces):
        value_piece, shell_piece, mu_piece = pieces
        mu_hot = (mu_piece[None, :] == jnp.arange(MUBINS, dtype=jnp.int32)[:, None]).astype(jnp.float32)
        rows = (value_piece[:, None, :] * mu_hot[None]).reshape(3 * MUBINS, block)
        rows = jnp.concatenate([rows, mu_hot], axis=0)
        shell_hot = (shell_piece[None, :] == jnp.arange(SHELLS, dtype=jnp.int32)[:, None]).astype(jnp.float32)
        return (total + lax.dot_general(rows, shell_hot, (((1,), (1,)), ((), ())), precision=lax.Precision.HIGHEST), None)
    start = jnp.zeros((4 * MUBINS, SHELLS), jnp.float32)
    total, _ = lax.scan(step, start, (value_blocks, shell_blocks, mu_blocks))
    return total

def reference(fields, shells, mubins):
    group = FIELDS // N_FIELD
    cos_table, sin_table = dft_tables(NZ)
    cos_wide = cos_table.astype(jnp.float32)
    sin_wide = sin_table.astype(jnp.float32)
    coef = jnp.asarray(make_coef())
    depth = jnp.arange(NZ, dtype=jnp.int32)
    wave_z = jnp.where(depth >= NZ // 2, depth - NZ, depth).astype(jnp.float32)
    wave_y = (NZ // 8 + jnp.arange(YROWS, dtype=jnp.int32)).astype(jnp.float32)

    def plane(total, plane_index):
        data = lax.dynamic_index_in_dim(fields, plane_index, 3, keepdims=False)
        flat = data.astype(jnp.float32).reshape(NZ, 2 * FIELDS * YROWS)
        first = jnp.dot(cos_wide, flat, precision=lax.Precision.HIGHEST).reshape(NZ, 2, FIELDS, YROWS)
        second = jnp.dot(sin_wide, flat, precision=lax.Precision.HIGHEST).reshape(NZ, 2, FIELDS, YROWS)
        real_part = first[:, 0] + second[:, 1]
        imag_part = first[:, 1] - second[:, 0]
        cross = real_part[:, :1] * real_part + imag_part[:, :1] * imag_part
        wave_x = (NZ // 4 + plane_index).astype(jnp.float32)
        terms = monomials(wave_x + jnp.zeros((NZ, YROWS), jnp.float32), wave_y[None, :], wave_z[:, None])
        weights = jnp.einsum('maj,jzy->mazy', coef, terms, precision=lax.Precision.HIGHEST)
        contrib = weights * jnp.transpose(cross, (1, 0, 2))[None]
        per_group = contrib.reshape(3, N_FIELD, group, NZ, YROWS).sum(axis=2)
        rounded = lax.optimization_barrier(per_group.astype(jnp.bfloat16)).astype(jnp.float32)
        cell_values = rounded.sum(axis=1).reshape(3, NZ * YROWS)
        shell_ids = lax.dynamic_index_in_dim(shells, plane_index, 1, keepdims=False).reshape(NZ * YROWS)
        mu_ids = lax.dynamic_index_in_dim(mubins, plane_index, 1, keepdims=False).reshape(NZ * YROWS)
        return (total + bin_cells(cell_values, shell_ids, mu_ids), None)
    start = jnp.zeros((4 * MUBINS, SHELLS), jnp.float32)
    total, _ = lax.scan(plane, start, jnp.arange(PLANES, dtype=jnp.int32))
    sums = total[:3 * MUBINS].reshape(3, MUBINS, SHELLS)
    counts = total[3 * MUBINS:]
    return sums / jnp.maximum(counts, 1.0)[None]
```

```python
import math

import jax
import jax.numpy as jnp
import numpy as np
from jax import lax
from jax.experimental import pallas as pl
from jax.experimental.pallas import tpu as pltpu
from jax.sharding import PartitionSpec as P

NZ = 2048
HALF = NZ // 2
SHELLS = 256
MUBINS = 8
PLANES = 16
YROWS = 256
COLS = 32
ROWS = 72
TK = 256
BOTH = ("field", "gz")


def dft_tables():
    index = np.arange(NZ, dtype=np.int64)
    product = (np.arange(HALF + 1, dtype=np.int64)[:, None] * index[None, :]) % NZ
    angle = (product.astype(np.float32) * np.float32(2.0 * math.pi / NZ)).astype(np.float64)
    factor = np.float32(1.0 / math.sqrt(NZ))
    cos_rows = (np.cos(angle).astype(np.float32) * factor).astype(jnp.bfloat16)
    sin_rows = (np.sin(angle).astype(np.float32) * factor).astype(jnp.bfloat16)
    sin_rows[0] = cos_rows[HALF]
    return cos_rows[:HALF], sin_rows[:HALF]


def swap_groups(parts, lane):
    upper = lane >= 64
    odd = (lane & 32) != 0
    a, b, c, d = parts
    a, c = jnp.where(upper, pltpu.roll(c, 64, 1), a), jnp.where(upper, c, pltpu.roll(a, 64, 1))
    b, d = jnp.where(upper, pltpu.roll(d, 64, 1), b), jnp.where(upper, d, pltpu.roll(b, 64, 1))
    a, b = jnp.where(odd, pltpu.roll(b, 32, 1), a), jnp.where(odd, b, pltpu.roll(a, 96, 1))
    c, d = jnp.where(odd, pltpu.roll(d, 32, 1), c), jnp.where(odd, d, pltpu.roll(c, 96, 1))
    return a, b, c, d


def pack_kernel(place, fields_ref, shells_ref, mubins_ref, out_ref):
    step = pl.program_id(0)
    row = lax.broadcasted_iota(jnp.int32, (256, 256), 0)
    col = lax.broadcasted_iota(jnp.int32, (256, 256), 1)
    lane = lax.broadcasted_iota(jnp.int32, (256, 128), 1)
    order = (col == (row % 16) * 16 + row // 16).astype(jnp.bfloat16)
    parts = [
        jnp.dot(
            order,
            fields_ref[:, c, f].reshape(256, YROWS),
            preferred_element_type=jnp.float32,
        )
        for c in range(2)
        for f in range(2)
    ]
    start = pl.multiple_of(step * 16, 16)
    for half in range(2):
        quarters = swap_groups([part[:, half * 128 : half * 128 + 128] for part in parts], lane)
        for q in range(4):
            block = quarters[q].astype(jnp.bfloat16).reshape(16, 16, 128)
            for p in range(PLANES):
                out_ref[q * 32 + p * 2 + half, pl.ds(start, 16), :] = block[p]

    @pl.when(step == 3)
    def _():
        inner = row % 16
        inner = jnp.where(place[1] >= 16, 15 - inner, inner)
        turned = (col == inner * 16 + row // 16).astype(jnp.bfloat16)
        maps = [
            jnp.dot(
                turned,
                ref[...].reshape(256, YROWS).astype(jnp.bfloat16),
                preferred_element_type=jnp.float32,
            ).reshape(16, 2, 8, YROWS)
            for ref in (shells_ref, mubins_ref)
        ]
        groups = [item[:, h].reshape(128, YROWS) for item in maps for h in range(2)]
        for half in range(2):
            quarters = swap_groups([g[:, half * 128 : half * 128 + 128] for g in groups], lane[:128])
            for q in range(4):
                block = quarters[q].reshape(16, 8, 128)
                for p in range(PLANES):
                    out_ref[q * 32 + p * 2 + half, 64:72, :] = block[p].astype(jnp.bfloat16)


def pack(place, fields, shells, mubins):
    return pl.pallas_call(
        pack_kernel,
        grid_spec=pltpu.PrefetchScalarGridSpec(
            num_scalar_prefetch=1,
            grid=(4,),
            in_specs=[
                pl.BlockSpec((16, 2, 2, PLANES, YROWS), lambda i, place: (i, 0, 0, 0, 0)),
                pl.BlockSpec((16, PLANES, YROWS), lambda i, place: (place[2], 0, 0)),
                pl.BlockSpec((16, PLANES, YROWS), lambda i, place: (place[2], 0, 0)),
            ],
            out_specs=pl.BlockSpec((128, ROWS, 128), lambda i, place: (0, 0, 0)),
        ),
        out_shape=jax.ShapeDtypeStruct((128, ROWS, 128), jnp.bfloat16),
        compiler_params=pltpu.CompilerParams(vmem_limit_bytes=32 * 1024 * 1024),
        name="pack",
    )(place, fields, shells, mubins)


def fold(parts, lane, width):
    first, second = parts
    odd = (lane & width) != 0
    kept = jnp.where(odd, second, first)
    moved = jnp.where(odd, first, second)
    return kept + pltpu.roll(moved, width, 1) if width == 64 else kept + swap32(moved, lane)


def swap32(value, lane):
    odd = (lane & 32) != 0
    return jnp.where(odd, pltpu.roll(value, 32, 1), pltpu.roll(value, 96, 1))


def bins_kernel(place, recv_ref, cos_ref, sin_ref, out_ref, lines, low, high, real, turn, values, hot_v, hot_s, acc):
    step = pl.program_id(0)
    lane = lax.broadcasted_iota(jnp.int32, (8, 128), 1)
    sub = lax.broadcasted_iota(jnp.int32, (8, 128), 0)
    upper = lane >= 64
    odd = (lane & 32) != 0

    @pl.when(step == 0)
    def _():
        acc[...] = jnp.zeros_like(acc)
        for f in range(4):
            for j in range(32):
                lines[j * 64 : j * 64 + 64, f * 128 : f * 128 + 128] = recv_ref[f * 32 + j, 0:64, :]
        tiles = []
        for tile in range(64):
            turned = tile >= 32
            source = 31 - (tile - 32) // 2 if turned else tile // 2
            pair = (tile % 2) * 2
            one = recv_ref[pair * 32 + source, 64:72, :].astype(jnp.float32)
            two = recv_ref[(pair + 1) * 32 + source, 64:72, :].astype(jnp.float32)
            shell = jnp.where(upper, pltpu.roll(two, 64, 1), one)
            mu = jnp.where(upper, two, pltpu.roll(one, 64, 1))
            tiles.append(shell + 256.0 * mu)
        rolled = [pltpu.roll(t, 1, 0) for t in tiles[32:]]
        moved = [pltpu.roll(t, 32, 1) for t in rolled]
        for m in range(32):
            first = jnp.where(lane < 32, moved[m - 1], moved[m])
            tiles[32 + m] = jnp.where(sub == 0, first, rolled[m])
        for tile in range(64):
            top = jnp.floor(tiles[tile] * (1.0 / 128.0))
            at = ((tile % 32) * 2 + tile // 32) * 8
            high[at : at + 8, :] = top
            low[at : at + 8, :] = tiles[tile] - 128.0 * top

    real[...] = jnp.dot(cos_ref[...], lines[...], preferred_element_type=jnp.float32)
    turn[...] = jnp.dot(sin_ref[...], lines[...], preferred_element_type=jnp.float32)

    spot = place[1]
    col = (lane & 31).astype(jnp.float32)
    wave_x = (NZ // 4 + spot // 2).astype(jnp.float32)
    wave_y = (NZ // 8 + (spot % 2) * 128 + place[0] * 32).astype(jnp.float32) + col
    plane_square = wave_x * wave_x + wave_y * wave_y
    weight_one = jnp.where(odd, wave_y * wave_y, wave_x * wave_x) * 1.5
    mixed = wave_x * wave_y * 3.0
    linear = jnp.where(odd, wave_y, wave_x) * 3.0
    turn_sign = jnp.where(upper, -1.0, 1.0)
    step16 = lax.broadcasted_iota(jnp.int32, (16, 128), 0).astype(jnp.float32).astype(jnp.bfloat16)
    step128 = lax.broadcasted_iota(jnp.int32, (128, 128), 0).astype(jnp.float32).astype(jnp.bfloat16)

    def tile_body(m, carry):
        products = [[], []]
        for q in range(4):
            at = pl.multiple_of(m * 32 + q * 8, 8)
            k_row = step * TK + at + sub
            first = k_row == 0
            wave_z = k_row.astype(jnp.float32)
            for sign in range(2):
                kz = wave_z if sign == 0 else jnp.where(first, -float(HALF), -wave_z)
                square = kz * kz
                inverse = 1.0 / (plane_square + square)
                weights = (
                    None,
                    weight_one * inverse,
                    jnp.where(odd, mixed, 1.5 * square) * inverse,
                    linear * kz * inverse,
                )
                spectra = []
                for f in range(4):
                    a = real[pl.ds(at, 8), f * 128 : f * 128 + 128]
                    b = pltpu.roll(turn[pl.ds(at, 8), f * 128 : f * 128 + 128], 64, 1) * turn_sign
                    if sign == 0:
                        spectra.append(a + jnp.where(first, 0.0, b))
                    else:
                        spectra.append(jnp.where(first, 0.0, a) - b)
                base = jnp.where(odd, pltpu.roll(spectra[0], 32, 1), spectra[0])
                cross = [base * s for s in spectra]
                products[sign].append([cross[0]] + [cross[f] * weights[f] for f in (1, 2, 3)])
        for sign in range(2):
            quad = products[sign]
            pairs = [
                (fold((quad[0][f], quad[2][f]), lane, 64), fold((quad[1][f], quad[3][f]), lane, 64))
                for f in range(4)
            ]
            even, other = pairs[0]
            tiles = [
                jnp.where(odd, pltpu.roll(other, 32, 1), even),
                jnp.where(odd, other, pltpu.roll(even, 96, 1)),
            ] + [fold(pairs[f], lane, 32) for f in (1, 2, 3)]
            at = pl.multiple_of((step * (TK // 32) + m) * 16 + sign * 8, 8)
            lows = low[pl.ds(at, 8), :]
            highs = high[pl.ds(at, 8), :]
            for r in range(8):
                place_at = (sign * 8 + r) * 128
                spread = jnp.broadcast_to(highs[r : r + 1], (16, 128)).astype(jnp.bfloat16)
                hit = spread == step16
                for v in range(5):
                    item = jnp.broadcast_to(tiles[v][r : r + 1], (16, 128)).astype(jnp.bfloat16)
                    hot_v[v * 16 : v * 16 + 16, place_at : place_at + 128] = jnp.where(
                        hit, item, jnp.bfloat16(0)
                    )
                hot_v[80:96, place_at : place_at + 128] = jnp.where(hit, jnp.bfloat16(1), jnp.bfloat16(0))
                spread = jnp.broadcast_to(lows[r : r + 1], (16, 128)).astype(jnp.bfloat16)
                spread = jnp.concatenate([spread] * 8, axis=0)
                hot_s[:, place_at : place_at + 128] = jnp.where(
                    spread == step128, jnp.bfloat16(1), jnp.bfloat16(0)
                )
        acc[...] += lax.dot_general(
            hot_v[...], hot_s[...], (((1,), (1,)), ((), ())), preferred_element_type=jnp.float32
        )
        return carry

    lax.fori_loop(0, TK // 32, tile_body, 0)

    @pl.when(step == pl.num_programs(0) - 1)
    def _():
        out_ref[0:32, :] = acc[0:32, :]
        out_ref[32:48, :] = acc[32:48, :] + acc[48:64, :] + acc[64:80, :] - 0.5 * acc[16:32, :]
        out_ref[48:64, :] = acc[80:96, :]


def bins(place, received, cos_table, sin_table):
    return pl.pallas_call(
        bins_kernel,
        grid_spec=pltpu.PrefetchScalarGridSpec(
            num_scalar_prefetch=1,
            grid=(HALF // TK,),
            in_specs=[
                pl.BlockSpec((128, ROWS, 128), lambda i, place: (0, 0, 0)),
                pl.BlockSpec((TK, NZ), lambda i, place: (i, 0)),
                pl.BlockSpec((TK, NZ), lambda i, place: (i, 0)),
            ],
            out_specs=pl.BlockSpec((64, 128), lambda i, place: (0, 0)),
            scratch_shapes=[
                pltpu.VMEM((NZ, 512), jnp.bfloat16),
                pltpu.VMEM((512, 128), jnp.float32),
                pltpu.VMEM((512, 128), jnp.float32),
                pltpu.VMEM((TK, 512), jnp.float32),
                pltpu.VMEM((TK, 512), jnp.float32),
                pltpu.VMEM((8, 128), jnp.float32),
                pltpu.VMEM((96, 2048), jnp.bfloat16),
                pltpu.VMEM((128, 2048), jnp.bfloat16),
                pltpu.VMEM((96, 128), jnp.float32),
            ],
        ),
        out_shape=jax.ShapeDtypeStruct((64, 128), jnp.float32),
        compiler_params=pltpu.CompilerParams(vmem_limit_bytes=40 * 1024 * 1024),
        name="bins",
    )(place, received, cos_table, sin_table)


def total_over_devices(value):
    for axis, size, bit in (
        ("gz", 32, 1),
        ("gz", 32, 2),
        ("gz", 32, 8),
        ("field", 4, 1),
        ("gz", 32, 6),
        ("gz", 32, 24),
        ("field", 4, 3),
    ):
        value = value + lax.ppermute(value, axis, [(i, i ^ bit) for i in range(size)])
    return value


def body(fields, shells, mubins):
    field, spot = lax.axis_index("field"), lax.axis_index("gz")
    cos_table, sin_table = dft_tables()
    place = jnp.stack([field, spot, jnp.where(spot >= 16, 3 - field, field)]).astype(jnp.int32)
    sent = pack(place, fields, shells, mubins)
    received = lax.all_to_all(sent, BOTH, split_axis=0, concat_axis=0, tiled=True)
    partial = bins(place, received, jnp.asarray(cos_table), jnp.asarray(sin_table))
    total = total_over_devices(partial).reshape(4, MUBINS, SHELLS)
    return total[:3] / jnp.maximum(total[3], 1.0)[None]


def solution(mesh):
    in_specs = (P("gz", None, "field", None, None), P("gz", None, None), P("gz", None, None))
    return jax.shard_map(body, mesh=mesh, in_specs=in_specs, out_specs=P(), check_vma=False)
```

```python
import math

import jax
import jax.numpy as jnp
import numpy as np
from jax import lax
from jax.experimental import pallas as pl
from jax.experimental.pallas import tpu as pltpu
from jax.sharding import PartitionSpec as P

NZ = 2048
HALF = NZ // 2
SHELLS = 256
MUBINS = 8
PLANES = 16
YROWS = 256
COLS = 32
ROWS = 72
TK = 256
UNROLL = 8
BOTH = ("field", "gz")


def dft_tables():
    index = np.arange(NZ, dtype=np.int64)
    product = (np.arange(HALF + 1, dtype=np.int64)[:, None] * index[None, :]) % NZ
    angle = (product.astype(np.float32) * np.float32(2.0 * math.pi / NZ)).astype(np.float64)
    factor = np.float32(1.0 / math.sqrt(NZ))
    cos_rows = (np.cos(angle).astype(np.float32) * factor).astype(jnp.bfloat16)
    sin_rows = (np.sin(angle).astype(np.float32) * factor).astype(jnp.bfloat16)
    sin_rows[0] = cos_rows[HALF]
    return cos_rows[:HALF], sin_rows[:HALF]


def swap_groups(parts, lane):
    upper = lane >= 64
    odd = (lane & 32) != 0
    a, b, c, d = parts
    a, c = jnp.where(upper, pltpu.roll(c, 64, 1), a), jnp.where(upper, c, pltpu.roll(a, 64, 1))
    b, d = jnp.where(upper, pltpu.roll(d, 64, 1), b), jnp.where(upper, d, pltpu.roll(b, 64, 1))
    a, b = jnp.where(odd, pltpu.roll(b, 32, 1), a), jnp.where(odd, b, pltpu.roll(a, 96, 1))
    c, d = jnp.where(odd, pltpu.roll(d, 32, 1), c), jnp.where(odd, d, pltpu.roll(c, 96, 1))
    return a, b, c, d


def pack_kernel(place, fields_hbm, shells_hbm, mubins_hbm, out_ref, fields_ref, index_ref, field_sems, index_sems):
    spot = pl.multiple_of(place[2] * 16, 16)
    copies = [
        pltpu.make_async_copy(
            fields_hbm.at[pl.ds(part * 16, 16)], fields_ref.at[pl.ds(part * 16, 16)], field_sems.at[part]
        )
        for part in range(4)
    ]
    index_copies = [
        pltpu.make_async_copy(source.at[pl.ds(spot, 16)], index_ref.at[n], index_sems.at[n])
        for n, source in enumerate((shells_hbm, mubins_hbm))
    ]
    for copy in index_copies + copies:
        copy.start()
    row = lax.broadcasted_iota(jnp.int32, (256, 256), 0)
    col = lax.broadcasted_iota(jnp.int32, (256, 256), 1)
    lane = lax.broadcasted_iota(jnp.int32, (256, 128), 1)
    inner = row % 16
    order = (col == inner * 16 + row // 16).astype(jnp.bfloat16)
    turned = jnp.where(place[1] >= 16, 15 - inner, inner)
    turned = (col == turned * 16 + row // 16).astype(jnp.bfloat16)

    for copy in index_copies:
        copy.wait()
    maps = [
        jnp.dot(
            turned,
            index_ref[n].reshape(256, YROWS).astype(jnp.bfloat16),
            preferred_element_type=jnp.float32,
        ).reshape(16, 2, 8, YROWS)
        for n in range(2)
    ]
    groups = [item[:, h].reshape(128, YROWS) for item in maps for h in range(2)]
    for half in range(2):
        quarters = swap_groups([g[:, half * 128 : half * 128 + 128] for g in groups], lane[:128])
        for q in range(4):
            block = quarters[q].reshape(16, 8, 128)
            for p in range(PLANES):
                out_ref[q * 32 + p * 2 + half, 64:72, :] = block[p].astype(jnp.bfloat16)

    for part in range(4):
        copies[part].wait()
        start = part * 16
        parts = [
            jnp.dot(
                order,
                fields_ref[start : start + 16, c, f].reshape(256, YROWS),
                preferred_element_type=jnp.float32,
            )
            for c in range(2)
            for f in range(2)
        ]
        for half in range(2):
            quarters = swap_groups([item[:, half * 128 : half * 128 + 128] for item in parts], lane)
            for q in range(4):
                block = quarters[q].astype(jnp.bfloat16).reshape(16, 16, 128)
                for p in range(PLANES):
                    out_ref[q * 32 + p * 2 + half, start : start + 16, :] = block[p]


def pack(place, fields, shells, mubins):
    return pl.pallas_call(
        pack_kernel,
        in_specs=[pl.BlockSpec(memory_space=pltpu.SMEM)] + [pl.BlockSpec(memory_space=pltpu.HBM)] * 3,
        out_specs=pl.BlockSpec(memory_space=pltpu.VMEM),
        scratch_shapes=[
            pltpu.VMEM((64, 2, 2, PLANES, YROWS), jnp.bfloat16),
            pltpu.VMEM((2, 16, PLANES, YROWS), jnp.int32),
            pltpu.SemaphoreType.DMA((4,)),
            pltpu.SemaphoreType.DMA((2,)),
        ],
        out_shape=jax.ShapeDtypeStruct((128, ROWS, 128), jnp.bfloat16),
        compiler_params=pltpu.CompilerParams(vmem_limit_bytes=32 * 1024 * 1024),
        name="pack",
    )(place, *[pltpu.with_memory_space_constraint(x, pltpu.HBM) for x in (fields, shells, mubins)])


def fold(parts, lane, width):
    first, second = parts
    odd = (lane & width) != 0
    kept = jnp.where(odd, second, first)
    moved = jnp.where(odd, first, second)
    return kept + pltpu.roll(moved, width, 1) if width == 64 else kept + swap32(moved, lane)


def swap32(value, lane):
    odd = (lane & 32) != 0
    return jnp.where(odd, pltpu.roll(value, 32, 1), pltpu.roll(value, 96, 1))


def bins_kernel(place, recv_ref, cos_ref, sin_ref, out_ref, lines, low, high, real, turn, acc):
    lane = lax.broadcasted_iota(jnp.int32, (8, 128), 1)
    sub = lax.broadcasted_iota(jnp.int32, (8, 128), 0)
    upper = lane >= 64
    odd = (lane & 32) != 0

    acc[...] = jnp.zeros_like(acc)
    for f in range(4):
        for j in range(32):
            lines[j * 64 : j * 64 + 64, f * 128 : f * 128 + 128] = recv_ref[f * 32 + j, 0:64, :]
    tiles = []
    for tile in range(64):
        turned = tile >= 32
        source = 31 - (tile - 32) // 2 if turned else tile // 2
        pair = (tile % 2) * 2
        one = recv_ref[pair * 32 + source, 64:72, :].astype(jnp.float32)
        two = recv_ref[(pair + 1) * 32 + source, 64:72, :].astype(jnp.float32)
        shell = jnp.where(upper, pltpu.roll(two, 64, 1), one)
        mu = jnp.where(upper, two, pltpu.roll(one, 64, 1))
        tiles.append(shell + 256.0 * mu)
    rolled = [pltpu.roll(t, 1, 0) for t in tiles[32:]]
    moved = [pltpu.roll(t, 32, 1) for t in rolled]
    for m in range(32):
        first = jnp.where(lane < 32, moved[m - 1], moved[m])
        tiles[32 + m] = jnp.where(sub == 0, first, rolled[m])
    for tile in range(64):
        top = jnp.floor(tiles[tile] * (1.0 / 128.0))
        at = ((tile % 32) * 2 + tile // 32) * 8
        high[at : at + 8, :] = top
        low[at : at + 8, :] = tiles[tile] - 128.0 * top

    for part in range(HALF // TK):
        rows = slice(part * TK, part * TK + TK)
        real[rows, :] = jnp.dot(cos_ref[rows, :], lines[...], preferred_element_type=jnp.float32)
        turn[rows, :] = jnp.dot(sin_ref[rows, :], lines[...], preferred_element_type=jnp.float32)

    spot = place[1]
    col = (lane & 31).astype(jnp.float32)
    wave_x = (NZ // 4 + spot // 2).astype(jnp.float32)
    wave_y = (NZ // 8 + (spot % 2) * 128 + place[0] * 32).astype(jnp.float32) + col
    plane_square = wave_x * wave_x + wave_y * wave_y
    weight_one = jnp.where(odd, wave_y * wave_y, wave_x * wave_x) * 1.5
    mixed = wave_x * wave_y * 3.0
    linear = jnp.where(odd, wave_y, wave_x) * 3.0
    turn_sign = jnp.where(upper, -1.0, 1.0)
    step16 = lax.broadcasted_iota(jnp.int32, (16, 128), 0).astype(jnp.float32).astype(jnp.bfloat16)
    step128 = lax.broadcasted_iota(jnp.int32, (128, 128), 0).astype(jnp.float32).astype(jnp.bfloat16)

    def tile_body(m, carry):
        products = [[], []]
        for q in range(4):
            at = pl.multiple_of(m * 32 + q * 8, 8)
            k_row = at + sub
            first = k_row == 0
            wave_z = k_row.astype(jnp.float32)
            for sign in range(2):
                kz = wave_z if sign == 0 else jnp.where(first, -float(HALF), -wave_z)
                square = kz * kz
                inverse = 1.0 / (plane_square + square)
                weights = (
                    None,
                    weight_one * inverse,
                    jnp.where(odd, mixed, 1.5 * square) * inverse,
                    linear * kz * inverse,
                )
                spectra = []
                for f in range(4):
                    a = real[pl.ds(at, 8), f * 128 : f * 128 + 128]
                    b = pltpu.roll(turn[pl.ds(at, 8), f * 128 : f * 128 + 128], 64, 1) * turn_sign
                    if sign == 0:
                        spectra.append(a + jnp.where(first, 0.0, b))
                    else:
                        spectra.append(jnp.where(first, 0.0, a) - b)
                base = jnp.where(odd, pltpu.roll(spectra[0], 32, 1), spectra[0])
                cross = [base * s for s in spectra]
                products[sign].append([cross[0]] + [cross[f] * weights[f] for f in (1, 2, 3)])
        for sign in range(2):
            quad = products[sign]
            pairs = [
                (fold((quad[0][f], quad[2][f]), lane, 64), fold((quad[1][f], quad[3][f]), lane, 64))
                for f in range(4)
            ]
            even, other = pairs[0]
            tiles = [
                jnp.where(odd, pltpu.roll(other, 32, 1), even),
                jnp.where(odd, other, pltpu.roll(even, 96, 1)),
            ] + [fold(pairs[f], lane, 32) for f in (1, 2, 3)]
            at = pl.multiple_of(m * 16 + sign * 8, 8)
            lows = low[pl.ds(at, 8), :]
            highs = high[pl.ds(at, 8), :]
            total = None
            for r0 in range(0, 8, 4):
                vals, hots = [], []
                for r in range(r0, r0 + 4):
                    spread = jnp.broadcast_to(highs[r : r + 1], (16, 128)).astype(jnp.bfloat16)
                    hit = spread == step16
                    items = [jnp.broadcast_to(tiles[v][r : r + 1], (16, 128)).astype(jnp.bfloat16) for v in range(5)]
                    vals.append(jnp.concatenate(
                        [jnp.where(hit, item, jnp.bfloat16(0)) for item in items]
                        + [jnp.where(hit, jnp.bfloat16(1), jnp.bfloat16(0))], axis=0))
                    spread = jnp.broadcast_to(lows[r : r + 1], (16, 128)).astype(jnp.bfloat16)
                    hots.append(jnp.where(jnp.concatenate([spread] * 8, axis=0) == step128, jnp.bfloat16(1), jnp.bfloat16(0)))
                part = lax.dot_general(
                    jnp.concatenate(vals, axis=1), jnp.concatenate(hots, axis=1),
                    (((1,), (1,)), ((), ())), preferred_element_type=jnp.float32)
                total = part if total is None else total + part
            acc[...] += total
        return carry

    lax.fori_loop(0, HALF // 32, tile_body, 0, unroll=UNROLL)

    out_ref[0:32, :] = acc[0:32, :]
    out_ref[32:48, :] = acc[32:48, :] + acc[48:64, :] + acc[64:80, :] - 0.5 * acc[16:32, :]
    out_ref[48:64, :] = acc[80:96, :]


def bins(place, received, cos_table, sin_table):
    return pl.pallas_call(
        bins_kernel,
        in_specs=[pl.BlockSpec(memory_space=pltpu.SMEM)] + [pl.BlockSpec(memory_space=pltpu.VMEM)] * 3,
        out_specs=pl.BlockSpec(memory_space=pltpu.VMEM),
        scratch_shapes=[
            pltpu.VMEM((NZ, 512), jnp.bfloat16),
            pltpu.VMEM((512, 128), jnp.float32),
            pltpu.VMEM((512, 128), jnp.float32),
            pltpu.VMEM((HALF, 512), jnp.float32),
            pltpu.VMEM((HALF, 512), jnp.float32),
            pltpu.VMEM((96, 128), jnp.float32),
        ],
        out_shape=jax.ShapeDtypeStruct((64, 128), jnp.float32),
        compiler_params=pltpu.CompilerParams(vmem_limit_bytes=40 * 1024 * 1024),
        name="bins",
    )(place, received, cos_table, sin_table)


def total_over_devices(value):
    for bits in (1, 3, 9, 33, 7, 25, 97):
        value = value + lax.ppermute(value, BOTH, [(i, i ^ bits) for i in range(128)])
    return value


def body(fields, shells, mubins):
    field, spot = lax.axis_index("field"), lax.axis_index("gz")
    cos_table, sin_table = dft_tables()
    place = jnp.stack([field, spot, jnp.where(spot >= 16, 3 - field, field)]).astype(jnp.int32)
    sent = pack(place, fields, shells, mubins)
    received = lax.all_to_all(sent, BOTH, split_axis=0, concat_axis=0, tiled=True)
    partial = bins(place, received, jnp.asarray(cos_table), jnp.asarray(sin_table))
    total = total_over_devices(partial).reshape(4, MUBINS, SHELLS)
    return total[:3] / jnp.maximum(total[3], 1.0)[None]


def solution(mesh):
    in_specs = (P("gz", None, "field", None, None), P("gz", None, None), P("gz", None, None))
    return jax.shard_map(body, mesh=mesh, in_specs=in_specs, out_specs=P(), check_vma=False)
```

```python
import math

import jax
import jax.numpy as jnp
import numpy as np
from jax import lax
from jax.experimental import pallas as pl
from jax.experimental.pallas import tpu as pltpu
from jax.sharding import PartitionSpec as P

NZ = 2048
HALF = NZ // 2
SHELLS = 256
MUBINS = 8
PLANES = 16
YROWS = 256
COLS = 32
ROWS = 72
TK = 256
UNROLL = 16
BOTH = ("field", "gz")


def dft_tables():
    index = np.arange(NZ, dtype=np.int64)
    product = (np.arange(HALF + 1, dtype=np.int64)[:, None] * index[None, :]) % NZ
    angle = (product.astype(np.float32) * np.float32(2.0 * math.pi / NZ)).astype(np.float64)
    factor = np.float32(1.0 / math.sqrt(NZ))
    cos_rows = (np.cos(angle).astype(np.float32) * factor).astype(jnp.bfloat16)
    sin_rows = (np.sin(angle).astype(np.float32) * factor).astype(jnp.bfloat16)
    sin_rows[0] = cos_rows[HALF]
    return cos_rows[:HALF], sin_rows[:HALF]


def swap_groups(parts, lane):
    upper = lane >= 64
    odd = (lane & 32) != 0
    a, b, c, d = parts
    a, c = jnp.where(upper, pltpu.roll(c, 64, 1), a), jnp.where(upper, c, pltpu.roll(a, 64, 1))
    b, d = jnp.where(upper, pltpu.roll(d, 64, 1), b), jnp.where(upper, d, pltpu.roll(b, 64, 1))
    a, b = jnp.where(odd, pltpu.roll(b, 32, 1), a), jnp.where(odd, b, pltpu.roll(a, 96, 1))
    c, d = jnp.where(odd, pltpu.roll(d, 32, 1), c), jnp.where(odd, d, pltpu.roll(c, 96, 1))
    return a, b, c, d


def pack_kernel(place, fields_hbm, shells_hbm, mubins_hbm, out_ref, fields_ref, index_ref, field_sems, index_sems):
    spot = pl.multiple_of(place[2] * 16, 16)
    copies = [
        pltpu.make_async_copy(
            fields_hbm.at[pl.ds(part * 16, 16)], fields_ref.at[pl.ds(part * 16, 16)], field_sems.at[part]
        )
        for part in range(4)
    ]
    index_copies = [
        pltpu.make_async_copy(source.at[pl.ds(spot, 16)], index_ref.at[n], index_sems.at[n])
        for n, source in enumerate((shells_hbm, mubins_hbm))
    ]
    for copy in copies + index_copies:
        copy.start()
    row = lax.broadcasted_iota(jnp.int32, (256, 256), 0)
    col = lax.broadcasted_iota(jnp.int32, (256, 256), 1)
    lane = lax.broadcasted_iota(jnp.int32, (256, 128), 1)
    inner = row % 16
    order = (col == inner * 16 + row // 16).astype(jnp.bfloat16)
    turned = jnp.where(place[1] >= 16, 15 - inner, inner)
    turned = (col == turned * 16 + row // 16).astype(jnp.bfloat16)

    for part in range(4):
        copies[part].wait()
        start = part * 16
        parts = [
            jnp.dot(
                order,
                fields_ref[start : start + 16, c, f].reshape(256, YROWS),
                preferred_element_type=jnp.float32,
            )
            for c in range(2)
            for f in range(2)
        ]
        for half in range(2):
            quarters = swap_groups([item[:, half * 128 : half * 128 + 128] for item in parts], lane)
            for q in range(4):
                block = quarters[q].astype(jnp.bfloat16).reshape(16, 16, 128)
                for p in range(PLANES):
                    out_ref[q * 32 + p * 2 + half, start : start + 16, :] = block[p]

    for copy in index_copies:
        copy.wait()
    maps = [
        jnp.dot(
            turned,
            index_ref[n].reshape(256, YROWS).astype(jnp.bfloat16),
            preferred_element_type=jnp.float32,
        ).reshape(16, 2, 8, YROWS)
        for n in range(2)
    ]
    groups = [item[:, h].reshape(128, YROWS) for item in maps for h in range(2)]
    for half in range(2):
        quarters = swap_groups([g[:, half * 128 : half * 128 + 128] for g in groups], lane[:128])
        for q in range(4):
            block = quarters[q].reshape(16, 8, 128)
            for p in range(PLANES):
                out_ref[q * 32 + p * 2 + half, 64:72, :] = block[p].astype(jnp.bfloat16)


def pack(place, fields, shells, mubins):
    return pl.pallas_call(
        pack_kernel,
        in_specs=[pl.BlockSpec(memory_space=pltpu.SMEM)] + [pl.BlockSpec(memory_space=pltpu.HBM)] * 3,
        out_specs=pl.BlockSpec(memory_space=pltpu.VMEM),
        scratch_shapes=[
            pltpu.VMEM((64, 2, 2, PLANES, YROWS), jnp.bfloat16),
            pltpu.VMEM((2, 16, PLANES, YROWS), jnp.int32),
            pltpu.SemaphoreType.DMA((4,)),
            pltpu.SemaphoreType.DMA((2,)),
        ],
        out_shape=jax.ShapeDtypeStruct((128, ROWS, 128), jnp.bfloat16),
        compiler_params=pltpu.CompilerParams(vmem_limit_bytes=32 * 1024 * 1024),
        name="pack",
    )(place, *[pltpu.with_memory_space_constraint(x, pltpu.HBM) for x in (fields, shells, mubins)])


def fold(parts, lane, width):
    first, second = parts
    odd = (lane & width) != 0
    kept = jnp.where(odd, second, first)
    moved = jnp.where(odd, first, second)
    return kept + pltpu.roll(moved, width, 1) if width == 64 else kept + swap32(moved, lane)


def swap32(value, lane):
    odd = (lane & 32) != 0
    return jnp.where(odd, pltpu.roll(value, 32, 1), pltpu.roll(value, 96, 1))


def bins_kernel(place, recv_ref, cos_ref, sin_ref, out_ref, lines, low, high, real, turn, acc):
    lane = lax.broadcasted_iota(jnp.int32, (8, 128), 1)
    sub = lax.broadcasted_iota(jnp.int32, (8, 128), 0)
    upper = lane >= 64
    odd = (lane & 32) != 0

    acc[...] = jnp.zeros_like(acc)
    for f in range(4):
        for j in range(32):
            lines[j * 64 : j * 64 + 64, f * 128 : f * 128 + 128] = recv_ref[f * 32 + j, 0:64, :]
    tiles = []
    for tile in range(64):
        turned = tile >= 32
        source = 31 - (tile - 32) // 2 if turned else tile // 2
        pair = (tile % 2) * 2
        one = recv_ref[pair * 32 + source, 64:72, :].astype(jnp.float32)
        two = recv_ref[(pair + 1) * 32 + source, 64:72, :].astype(jnp.float32)
        shell = jnp.where(upper, pltpu.roll(two, 64, 1), one)
        mu = jnp.where(upper, two, pltpu.roll(one, 64, 1))
        tiles.append(shell + 256.0 * mu)
    rolled = [pltpu.roll(t, 1, 0) for t in tiles[32:]]
    moved = [pltpu.roll(t, 32, 1) for t in rolled]
    for m in range(32):
        first = jnp.where(lane < 32, moved[m - 1], moved[m])
        tiles[32 + m] = jnp.where(sub == 0, first, rolled[m])
    for tile in range(64):
        top = jnp.floor(tiles[tile] * (1.0 / 128.0))
        at = ((tile % 32) * 2 + tile // 32) * 8
        high[at : at + 8, :] = top
        low[at : at + 8, :] = tiles[tile] - 128.0 * top

    for part in range(HALF // TK):
        rows = slice(part * TK, part * TK + TK)
        real[rows, :] = jnp.dot(cos_ref[rows, :], lines[...], preferred_element_type=jnp.float32)
        turn[rows, :] = jnp.dot(sin_ref[rows, :], lines[...], preferred_element_type=jnp.float32)

    spot = place[1]
    col = (lane & 31).astype(jnp.float32)
    wave_x = (NZ // 4 + spot // 2).astype(jnp.float32)
    wave_y = (NZ // 8 + (spot % 2) * 128 + place[0] * 32).astype(jnp.float32) + col
    plane_square = wave_x * wave_x + wave_y * wave_y
    weight_one = jnp.where(odd, wave_y * wave_y, wave_x * wave_x) * 1.5
    mixed = wave_x * wave_y * 3.0
    linear = jnp.where(odd, wave_y, wave_x) * 3.0
    turn_sign = jnp.where(upper, -1.0, 1.0)
    step16 = lax.broadcasted_iota(jnp.int32, (16, 128), 0).astype(jnp.float32).astype(jnp.bfloat16)
    step128 = lax.broadcasted_iota(jnp.int32, (128, 128), 0).astype(jnp.float32).astype(jnp.bfloat16)

    last_inverse = 1.0 / (plane_square + float(HALF) * HALF)
    for f in range(4):
        at = slice(f * 128, f * 128 + 128)
        a, b = real[0:8, at], pltpu.roll(turn[0:8, at], 64, 1) * turn_sign
        real[0:8, at] = jnp.where(sub == 0, 0.5 * (a - b), a)
        turn[0:8, at] = pltpu.roll(jnp.where(sub == 0, 0.5 * (a + b), b) * turn_sign, 64, 1)

    def tile_body(m, carry):
        products = [[], []]
        for q in range(4):
            at = pl.multiple_of(m * 32 + q * 8, 8)
            k_row = at + sub
            first = k_row == 0
            wave_z = k_row.astype(jnp.float32)
            plain_square = wave_z * wave_z
            plain_inverse = 1.0 / (plane_square + plain_square)
            for sign in range(2):
                kz = wave_z if sign == 0 else jnp.where(first, -float(HALF), -wave_z)
                square = plain_square if sign == 0 else jnp.where(first, float(HALF) * HALF, plain_square)
                inverse = plain_inverse if sign == 0 else jnp.where(first, last_inverse, plain_inverse)
                weights = (
                    None,
                    weight_one * inverse,
                    jnp.where(odd, mixed, 1.5 * square) * inverse,
                    linear * kz * inverse,
                )
                spectra = []
                for f in range(4):
                    a = real[pl.ds(at, 8), f * 128 : f * 128 + 128]
                    b = pltpu.roll(turn[pl.ds(at, 8), f * 128 : f * 128 + 128], 64, 1) * turn_sign
                    spectra.append(a + b if sign == 0 else a - b)
                base = jnp.where(odd, pltpu.roll(spectra[0], 32, 1), spectra[0])
                cross = [base * s for s in spectra]
                products[sign].append([cross[0]] + [cross[f] * weights[f] for f in (1, 2, 3)])
        for sign in range(2):
            quad = products[sign]
            pairs = [
                (fold((quad[0][f], quad[2][f]), lane, 64), fold((quad[1][f], quad[3][f]), lane, 64))
                for f in range(4)
            ]
            even, other = pairs[0]
            tiles = [
                jnp.where(odd, pltpu.roll(other, 32, 1), even),
                jnp.where(odd, other, pltpu.roll(even, 96, 1)),
            ] + [fold(pairs[f], lane, 32) for f in (1, 2, 3)]
            at = pl.multiple_of(m * 16 + sign * 8, 8)
            lows = low[pl.ds(at, 8), :]
            highs = high[pl.ds(at, 8), :]
            total = None
            for r0 in range(0, 8, 4):
                vals, hots = [], []
                for r in range(r0, r0 + 4):
                    spread = jnp.broadcast_to(highs[r : r + 1], (16, 128)).astype(jnp.bfloat16)
                    hit = spread == step16
                    items = [jnp.broadcast_to(tiles[v][r : r + 1], (16, 128)).astype(jnp.bfloat16) for v in range(5)]
                    vals.append(jnp.concatenate(
                        [jnp.where(hit, item, jnp.bfloat16(0)) for item in items]
                        + [jnp.where(hit, jnp.bfloat16(1), jnp.bfloat16(0))], axis=0))
                    spread = jnp.broadcast_to(lows[r : r + 1], (16, 128)).astype(jnp.bfloat16)
                    hots.append(jnp.where(jnp.concatenate([spread] * 8, axis=0) == step128, jnp.bfloat16(1), jnp.bfloat16(0)))
                part = lax.dot_general(
                    jnp.concatenate(vals, axis=1), jnp.concatenate(hots, axis=1),
                    (((1,), (1,)), ((), ())), preferred_element_type=jnp.float32)
                total = part if total is None else total + part
            acc[...] += total
        return carry

    lax.fori_loop(0, HALF // 32, tile_body, 0, unroll=UNROLL)

    out_ref[0:32, :] = acc[0:32, :]
    out_ref[32:48, :] = acc[32:48, :] + acc[48:64, :] + acc[64:80, :] - 0.5 * acc[16:32, :]
    out_ref[48:64, :] = acc[80:96, :]


def bins(place, received, cos_table, sin_table):
    return pl.pallas_call(
        bins_kernel,
        in_specs=[pl.BlockSpec(memory_space=pltpu.SMEM)] + [pl.BlockSpec(memory_space=pltpu.VMEM)] * 3,
        out_specs=pl.BlockSpec(memory_space=pltpu.VMEM),
        scratch_shapes=[
            pltpu.VMEM((NZ, 512), jnp.bfloat16),
            pltpu.VMEM((512, 128), jnp.float32),
            pltpu.VMEM((512, 128), jnp.float32),
            pltpu.VMEM((HALF, 512), jnp.float32),
            pltpu.VMEM((HALF, 512), jnp.float32),
            pltpu.VMEM((96, 128), jnp.float32),
        ],
        out_shape=jax.ShapeDtypeStruct((64, 128), jnp.float32),
        compiler_params=pltpu.CompilerParams(vmem_limit_bytes=40 * 1024 * 1024),
        name="bins",
    )(place, received, cos_table, sin_table)


def total_over_devices(value):
    for bits in (1, 3, 9, 33, 7, 25, 97):
        value = value + lax.ppermute(value, BOTH, [(i, i ^ bits) for i in range(128)])
    return value


def body(fields, shells, mubins):
    field, spot = lax.axis_index("field"), lax.axis_index("gz")
    cos_table, sin_table = dft_tables()
    place = jnp.stack([field, spot, jnp.where(spot >= 16, 3 - field, field)]).astype(jnp.int32)
    sent = pack(place, fields, shells, mubins)
    received = lax.all_to_all(sent, BOTH, split_axis=0, concat_axis=0, tiled=True)
    partial = bins(place, received, jnp.asarray(cos_table), jnp.asarray(sin_table))
    total = total_over_devices(partial).reshape(4, MUBINS, SHELLS)
    return total[:3] / jnp.maximum(total[3], 1.0)[None]


def solution(mesh):
    in_specs = (P("gz", None, "field", None, None), P("gz", None, None), P("gz", None, None))
    return jax.shard_map(body, mesh=mesh, in_specs=in_specs, out_specs=P(), check_vma=False)
```

```python
import math

import jax
import jax.numpy as jnp
import numpy as np
from jax import lax
from jax.experimental import pallas as pl
from jax.experimental.pallas import tpu as pltpu
from jax.sharding import PartitionSpec as P

NZ = 2048
HALF = NZ // 2
SHELLS = 256
MUBINS = 8
PLANES = 16
YROWS = 256
COLS = 32
ROWS = 72
TK = 256
UNROLL = 16
BOTH = ("field", "gz")


def dft_tables():
    index = np.arange(NZ, dtype=np.int64)
    product = (np.arange(HALF + 1, dtype=np.int64)[:, None] * index[None, :]) % NZ
    angle = (product.astype(np.float32) * np.float32(2.0 * math.pi / NZ)).astype(np.float64)
    factor = np.float32(1.0 / math.sqrt(NZ))
    cos_rows = (np.cos(angle).astype(np.float32) * factor).astype(jnp.bfloat16)
    sin_rows = (np.sin(angle).astype(np.float32) * factor).astype(jnp.bfloat16)
    sin_rows[0] = cos_rows[HALF]
    return cos_rows[:HALF], sin_rows[:HALF]


def swap_groups(parts, lane):
    upper = lane >= 64
    odd = (lane & 32) != 0
    a, b, c, d = parts
    a, c = jnp.where(upper, pltpu.roll(c, 64, 1), a), jnp.where(upper, c, pltpu.roll(a, 64, 1))
    b, d = jnp.where(upper, pltpu.roll(d, 64, 1), b), jnp.where(upper, d, pltpu.roll(b, 64, 1))
    a, b = jnp.where(odd, pltpu.roll(b, 32, 1), a), jnp.where(odd, b, pltpu.roll(a, 96, 1))
    c, d = jnp.where(odd, pltpu.roll(d, 32, 1), c), jnp.where(odd, d, pltpu.roll(c, 96, 1))
    return a, b, c, d


def pack_kernel(place, fields_hbm, shells_hbm, mubins_hbm, out_ref, fields_ref, index_ref, field_sems, index_sems):
    spot = pl.multiple_of(place[2] * 16, 16)
    copies = [
        pltpu.make_async_copy(
            fields_hbm.at[pl.ds(part * 16, 16)], fields_ref.at[pl.ds(part * 16, 16)], field_sems.at[part]
        )
        for part in range(4)
    ]
    index_copies = [
        pltpu.make_async_copy(source.at[pl.ds(spot, 16)], index_ref.at[n], index_sems.at[n])
        for n, source in enumerate((shells_hbm, mubins_hbm))
    ]
    queue = copies + index_copies
    queue[0].start()
    queue[1].start()
    row = lax.broadcasted_iota(jnp.int32, (256, 256), 0)
    col = lax.broadcasted_iota(jnp.int32, (256, 256), 1)
    lane = lax.broadcasted_iota(jnp.int32, (256, 128), 1)
    inner = row % 16
    order = (col == inner * 16 + row // 16).astype(jnp.bfloat16)
    turned = jnp.where(place[1] >= 16, 15 - inner, inner)
    turned = (col == turned * 16 + row // 16).astype(jnp.bfloat16)

    for part in range(4):
        copies[part].wait()
        queue[part + 2].start()
        start = part * 16
        parts = [
            jnp.dot(
                order,
                fields_ref[start : start + 16, c, f].reshape(256, YROWS),
                preferred_element_type=jnp.float32,
            )
            for c in range(2)
            for f in range(2)
        ]
        for half in range(2):
            quarters = swap_groups([item[:, half * 128 : half * 128 + 128] for item in parts], lane)
            for q in range(4):
                block = quarters[q].astype(jnp.bfloat16).reshape(16, 16, 128)
                for p in range(PLANES):
                    out_ref[q * 32 + p * 2 + half, start : start + 16, :] = block[p]

    for copy in index_copies:
        copy.wait()
    maps = [
        jnp.dot(
            turned,
            index_ref[n].reshape(256, YROWS).astype(jnp.bfloat16),
            preferred_element_type=jnp.float32,
        ).reshape(16, 2, 8, YROWS)
        for n in range(2)
    ]
    groups = [item[:, h].reshape(128, YROWS) for item in maps for h in range(2)]
    for half in range(2):
        quarters = swap_groups([g[:, half * 128 : half * 128 + 128] for g in groups], lane[:128])
        for q in range(4):
            block = quarters[q].reshape(16, 8, 128)
            for p in range(PLANES):
                out_ref[q * 32 + p * 2 + half, 64:72, :] = block[p].astype(jnp.bfloat16)


def pack(place, fields, shells, mubins):
    return pl.pallas_call(
        pack_kernel,
        in_specs=[pl.BlockSpec(memory_space=pltpu.SMEM)] + [pl.BlockSpec(memory_space=pltpu.HBM)] * 3,
        out_specs=pl.BlockSpec(memory_space=pltpu.VMEM),
        scratch_shapes=[
            pltpu.VMEM((64, 2, 2, PLANES, YROWS), jnp.bfloat16),
            pltpu.VMEM((2, 16, PLANES, YROWS), jnp.int32),
            pltpu.SemaphoreType.DMA((4,)),
            pltpu.SemaphoreType.DMA((2,)),
        ],
        out_shape=jax.ShapeDtypeStruct((128, ROWS, 128), jnp.bfloat16),
        compiler_params=pltpu.CompilerParams(vmem_limit_bytes=32 * 1024 * 1024),
        name="pack",
    )(place, *[pltpu.with_memory_space_constraint(x, pltpu.HBM) for x in (fields, shells, mubins)])


def fold(parts, lane, width):
    first, second = parts
    odd = (lane & width) != 0
    kept = jnp.where(odd, second, first)
    moved = jnp.where(odd, first, second)
    return kept + pltpu.roll(moved, width, 1) if width == 64 else kept + swap32(moved, lane)


def swap32(value, lane):
    odd = (lane & 32) != 0
    return jnp.where(odd, pltpu.roll(value, 32, 1), pltpu.roll(value, 96, 1))


def bins_kernel(place, recv_ref, cos_ref, sin_ref, out_ref, lines, low, high, real, turn, acc):
    lane = lax.broadcasted_iota(jnp.int32, (8, 128), 1)
    sub = lax.broadcasted_iota(jnp.int32, (8, 128), 0)
    upper = lane >= 64
    odd = (lane & 32) != 0

    acc[...] = jnp.zeros_like(acc)
    for f in range(4):
        for j in range(32):
            lines[j * 64 : j * 64 + 64, f * 128 : f * 128 + 128] = recv_ref[f * 32 + j, 0:64, :]
    tiles = []
    for tile in range(64):
        turned = tile >= 32
        source = 31 - (tile - 32) // 2 if turned else tile // 2
        pair = (tile % 2) * 2
        one = recv_ref[pair * 32 + source, 64:72, :].astype(jnp.float32)
        two = recv_ref[(pair + 1) * 32 + source, 64:72, :].astype(jnp.float32)
        shell = jnp.where(upper, pltpu.roll(two, 64, 1), one)
        mu = jnp.where(upper, two, pltpu.roll(one, 64, 1))
        tiles.append(shell + 256.0 * mu)
    rolled = [pltpu.roll(t, 1, 0) for t in tiles[32:]]
    moved = [pltpu.roll(t, 32, 1) for t in rolled]
    for m in range(32):
        first = jnp.where(lane < 32, moved[m - 1], moved[m])
        tiles[32 + m] = jnp.where(sub == 0, first, rolled[m])
    for tile in range(64):
        top = jnp.floor(tiles[tile] * (1.0 / 128.0))
        at = ((tile % 32) * 2 + tile // 32) * 8
        high[at : at + 8, :] = top
        low[at : at + 8, :] = tiles[tile] - 128.0 * top

    for part in range(HALF // TK):
        rows = slice(part * TK, part * TK + TK)
        real[rows, :] = jnp.dot(cos_ref[rows, :], lines[...], preferred_element_type=jnp.float32)
        turn[rows, :] = jnp.dot(sin_ref[rows, :], lines[...], preferred_element_type=jnp.float32)

    spot = place[1]
    col = (lane & 31).astype(jnp.float32)
    wave_x = (NZ // 4 + spot // 2).astype(jnp.float32)
    wave_y = (NZ // 8 + (spot % 2) * 128 + place[0] * 32).astype(jnp.float32) + col
    plane_square = wave_x * wave_x + wave_y * wave_y
    weight_one = jnp.where(odd, wave_y * wave_y, wave_x * wave_x) * 1.5
    mixed = wave_x * wave_y * 3.0
    linear = jnp.where(odd, wave_y, wave_x) * 3.0
    turn_sign = jnp.where(upper, -1.0, 1.0)
    step16 = lax.broadcasted_iota(jnp.int32, (16, 128), 0).astype(jnp.float32).astype(jnp.bfloat16)
    step128 = lax.broadcasted_iota(jnp.int32, (128, 128), 0).astype(jnp.float32).astype(jnp.bfloat16)

    last_inverse = 1.0 / (plane_square + float(HALF) * HALF)
    for f in range(4):
        at = slice(f * 128, f * 128 + 128)
        a, b = real[0:8, at], pltpu.roll(turn[0:8, at], 64, 1) * turn_sign
        real[0:8, at] = jnp.where(sub == 0, 0.5 * (a - b), a)
        turn[0:8, at] = pltpu.roll(jnp.where(sub == 0, 0.5 * (a + b), b) * turn_sign, 64, 1)

    def tile_body(m, carry):
        products = [[], []]
        for q in range(4):
            at = pl.multiple_of(m * 32 + q * 8, 8)
            k_row = at + sub
            first = k_row == 0
            wave_z = k_row.astype(jnp.float32)
            plain_square = wave_z * wave_z
            plain_inverse = 1.0 / (plane_square + plain_square)
            for sign in range(2):
                kz = wave_z if sign == 0 else jnp.where(first, -float(HALF), -wave_z)
                square = plain_square if sign == 0 else jnp.where(first, float(HALF) * HALF, plain_square)
                inverse = plain_inverse if sign == 0 else jnp.where(first, last_inverse, plain_inverse)
                weights = (
                    None,
                    weight_one * inverse,
                    jnp.where(odd, mixed, 1.5 * square) * inverse,
                    linear * kz * inverse,
                )
                spectra = []
                for f in range(4):
                    a = real[pl.ds(at, 8), f * 128 : f * 128 + 128]
                    b = pltpu.roll(turn[pl.ds(at, 8), f * 128 : f * 128 + 128], 64, 1) * turn_sign
                    spectra.append(a + b if sign == 0 else a - b)
                base = jnp.where(odd, pltpu.roll(spectra[0], 32, 1), spectra[0])
                cross = [base * s for s in spectra]
                products[sign].append([cross[0]] + [cross[f] * weights[f] for f in (1, 2, 3)])
        for sign in range(2):
            quad = products[sign]
            pairs = [
                (fold((quad[0][f], quad[2][f]), lane, 64), fold((quad[1][f], quad[3][f]), lane, 64))
                for f in range(4)
            ]
            even, other = pairs[0]
            tiles = [
                jnp.where(odd, pltpu.roll(other, 32, 1), even),
                jnp.where(odd, other, pltpu.roll(even, 96, 1)),
            ] + [fold(pairs[f], lane, 32) for f in (1, 2, 3)]
            at = pl.multiple_of(m * 16 + sign * 8, 8)
            lows = low[pl.ds(at, 8), :]
            highs = high[pl.ds(at, 8), :]
            total = None
            for r0 in range(0, 8, 4):
                vals, hots = [], []
                for r in range(r0, r0 + 4):
                    spread = jnp.broadcast_to(highs[r : r + 1], (16, 128)).astype(jnp.bfloat16)
                    hit = spread == step16
                    items = [jnp.broadcast_to(tiles[v][r : r + 1], (16, 128)).astype(jnp.bfloat16) for v in range(5)]
                    vals.append(jnp.concatenate(
                        [jnp.where(hit, item, jnp.bfloat16(0)) for item in items]
                        + [jnp.where(hit, jnp.bfloat16(1), jnp.bfloat16(0))], axis=0))
                    spread = jnp.broadcast_to(lows[r : r + 1], (16, 128)).astype(jnp.bfloat16)
                    hots.append(jnp.where(jnp.concatenate([spread] * 8, axis=0) == step128, jnp.bfloat16(1), jnp.bfloat16(0)))
                part = lax.dot_general(
                    jnp.concatenate(vals, axis=1), jnp.concatenate(hots, axis=1),
                    (((1,), (1,)), ((), ())), preferred_element_type=jnp.float32)
                total = part if total is None else total + part
            acc[...] += total
        return carry

    lax.fori_loop(0, HALF // 32, tile_body, 0, unroll=UNROLL)

    out_ref[0:32, :] = acc[0:32, :]
    out_ref[32:48, :] = acc[32:48, :] + acc[48:64, :] + acc[64:80, :] - 0.5 * acc[16:32, :]
    out_ref[48:64, :] = acc[80:96, :]


def bins(place, received, cos_table, sin_table):
    return pl.pallas_call(
        bins_kernel,
        in_specs=[pl.BlockSpec(memory_space=pltpu.SMEM)] + [pl.BlockSpec(memory_space=pltpu.VMEM)] * 3,
        out_specs=pl.BlockSpec(memory_space=pltpu.VMEM),
        scratch_shapes=[
            pltpu.VMEM((NZ, 512), jnp.bfloat16),
            pltpu.VMEM((512, 128), jnp.float32),
            pltpu.VMEM((512, 128), jnp.float32),
            pltpu.VMEM((HALF, 512), jnp.float32),
            pltpu.VMEM((HALF, 512), jnp.float32),
            pltpu.VMEM((96, 128), jnp.float32),
        ],
        out_shape=jax.ShapeDtypeStruct((64, 128), jnp.float32),
        compiler_params=pltpu.CompilerParams(vmem_limit_bytes=40 * 1024 * 1024),
        name="bins",
    )(place, received, cos_table, sin_table)


def total_over_devices(value):
    for bits in (1, 3, 9, 33, 7, 25, 97):
        value = value + lax.ppermute(value, BOTH, [(i, i ^ bits) for i in range(128)])
    return value


def body(fields, shells, mubins):
    field, spot = lax.axis_index("field"), lax.axis_index("gz")
    cos_table, sin_table = dft_tables()
    place = jnp.stack([field, spot, jnp.where(spot >= 16, 3 - field, field)]).astype(jnp.int32)
    sent = pack(place, fields, shells, mubins)
    received = lax.all_to_all(sent, BOTH, split_axis=0, concat_axis=0, tiled=True)
    partial = bins(place, received, jnp.asarray(cos_table), jnp.asarray(sin_table))
    total = total_over_devices(partial).reshape(4, MUBINS, SHELLS)
    return total[:3] / jnp.maximum(total[3], 1.0)[None]


def solution(mesh):
    in_specs = (P("gz", None, "field", None, None), P("gz", None, None), P("gz", None, None))
    return jax.shard_map(body, mesh=mesh, in_specs=in_specs, out_specs=P(), check_vma=False)
```

```python
import math

import jax
import jax.numpy as jnp
import numpy as np
from jax import lax
from jax.experimental import pallas as pl
from jax.experimental.pallas import tpu as pltpu
from jax.sharding import PartitionSpec as P

NZ = 2048
HALF = NZ // 2
SHELLS = 256
MUBINS = 8
PLANES = 16
YROWS = 256
COLS = 32
ROWS = 72
TK = 256
UNROLL = 16
BOTH = ("field", "gz")


def dft_tables():
    index = np.arange(NZ, dtype=np.int64)
    product = (np.arange(HALF + 1, dtype=np.int64)[:, None] * index[None, :]) % NZ
    angle = (product.astype(np.float32) * np.float32(2.0 * math.pi / NZ)).astype(np.float64)
    factor = np.float32(1.0 / math.sqrt(NZ))
    cos_rows = (np.cos(angle).astype(np.float32) * factor).astype(jnp.bfloat16)
    sin_rows = (np.sin(angle).astype(np.float32) * factor).astype(jnp.bfloat16)
    sin_rows[0] = cos_rows[HALF]
    return cos_rows[:HALF], sin_rows[:HALF]


def swap_groups(parts, lane):
    upper = lane >= 64
    odd = (lane & 32) != 0
    a, b, c, d = parts
    a, c = jnp.where(upper, pltpu.roll(c, 64, 1), a), jnp.where(upper, c, pltpu.roll(a, 64, 1))
    b, d = jnp.where(upper, pltpu.roll(d, 64, 1), b), jnp.where(upper, d, pltpu.roll(b, 64, 1))
    a, b = jnp.where(odd, pltpu.roll(b, 32, 1), a), jnp.where(odd, b, pltpu.roll(a, 96, 1))
    c, d = jnp.where(odd, pltpu.roll(d, 32, 1), c), jnp.where(odd, d, pltpu.roll(c, 96, 1))
    return a, b, c, d


def pack_kernel(place, fields_hbm, shells_hbm, mubins_hbm, out_ref, fields_ref, index_ref, field_sems, index_sems):
    spot = pl.multiple_of(place[2] * 16, 16)
    copies = [
        pltpu.make_async_copy(
            fields_hbm.at[pl.ds(part * 16, 16)], fields_ref.at[pl.ds(part * 16, 16)], field_sems.at[part]
        )
        for part in range(4)
    ]
    index_copies = [
        pltpu.make_async_copy(source.at[pl.ds(spot, 16)], index_ref.at[n], index_sems.at[n])
        for n, source in enumerate((shells_hbm, mubins_hbm))
    ]
    for copy in copies + index_copies:
        copy.start()
    row = lax.broadcasted_iota(jnp.int32, (256, 256), 0)
    col = lax.broadcasted_iota(jnp.int32, (256, 256), 1)
    lane = lax.broadcasted_iota(jnp.int32, (256, 128), 1)
    inner = row % 16
    order = (col == inner * 16 + row // 16).astype(jnp.bfloat16)
    turned = jnp.where(place[1] >= 16, 15 - inner, inner)
    turned = (col == turned * 16 + row // 16).astype(jnp.bfloat16)

    for part in range(4):
        if part == 0:
            copies[0].wait()
        if part == 1:
            for copy in copies[1:] + index_copies:
                copy.wait()
        start = part * 16
        parts = [
            jnp.dot(
                order,
                fields_ref[start : start + 16, c, f].reshape(256, YROWS),
                preferred_element_type=jnp.float32,
            )
            for c in range(2)
            for f in range(2)
        ]
        for half in range(2):
            quarters = swap_groups([item[:, half * 128 : half * 128 + 128] for item in parts], lane)
            for q in range(4):
                block = quarters[q].astype(jnp.bfloat16).reshape(16, 16, 128)
                for p in range(PLANES):
                    out_ref[q * 32 + p * 2 + half, start : start + 16, :] = block[p]

    maps = [
        jnp.dot(
            turned,
            index_ref[n].reshape(256, YROWS).astype(jnp.bfloat16),
            preferred_element_type=jnp.float32,
        ).reshape(16, 2, 8, YROWS)
        for n in range(2)
    ]
    groups = [item[:, h].reshape(128, YROWS) for item in maps for h in range(2)]
    for half in range(2):
        quarters = swap_groups([g[:, half * 128 : half * 128 + 128] for g in groups], lane[:128])
        for q in range(4):
            block = quarters[q].reshape(16, 8, 128)
            for p in range(PLANES):
                out_ref[q * 32 + p * 2 + half, 64:72, :] = block[p].astype(jnp.bfloat16)


def pack(place, fields, shells, mubins):
    return pl.pallas_call(
        pack_kernel,
        in_specs=[pl.BlockSpec(memory_space=pltpu.SMEM)] + [pl.BlockSpec(memory_space=pltpu.HBM)] * 3,
        out_specs=pl.BlockSpec(memory_space=pltpu.VMEM),
        scratch_shapes=[
            pltpu.VMEM((64, 2, 2, PLANES, YROWS), jnp.bfloat16),
            pltpu.VMEM((2, 16, PLANES, YROWS), jnp.int32),
            pltpu.SemaphoreType.DMA((4,)),
            pltpu.SemaphoreType.DMA((2,)),
        ],
        out_shape=jax.ShapeDtypeStruct((128, ROWS, 128), jnp.bfloat16),
        compiler_params=pltpu.CompilerParams(vmem_limit_bytes=32 * 1024 * 1024),
        name="pack",
    )(place, *[pltpu.with_memory_space_constraint(x, pltpu.HBM) for x in (fields, shells, mubins)])


def fold(parts, lane, width):
    first, second = parts
    odd = (lane & width) != 0
    kept = jnp.where(odd, second, first)
    moved = jnp.where(odd, first, second)
    return kept + pltpu.roll(moved, width, 1) if width == 64 else kept + swap32(moved, lane)


def swap32(value, lane):
    odd = (lane & 32) != 0
    return jnp.where(odd, pltpu.roll(value, 32, 1), pltpu.roll(value, 96, 1))


def bins_kernel(place, recv_ref, cos_ref, sin_ref, out_ref, lines, low, high, real, turn, acc):
    lane = lax.broadcasted_iota(jnp.int32, (8, 128), 1)
    sub = lax.broadcasted_iota(jnp.int32, (8, 128), 0)
    upper = lane >= 64
    odd = (lane & 32) != 0

    acc[...] = jnp.zeros_like(acc)
    for f in range(4):
        for j in range(32):
            lines[j * 64 : j * 64 + 64, f * 128 : f * 128 + 128] = recv_ref[f * 32 + j, 0:64, :]
    tiles = []
    for tile in range(64):
        turned = tile >= 32
        source = 31 - (tile - 32) // 2 if turned else tile // 2
        pair = (tile % 2) * 2
        one = recv_ref[pair * 32 + source, 64:72, :].astype(jnp.float32)
        two = recv_ref[(pair + 1) * 32 + source, 64:72, :].astype(jnp.float32)
        shell = jnp.where(upper, pltpu.roll(two, 64, 1), one)
        mu = jnp.where(upper, two, pltpu.roll(one, 64, 1))
        tiles.append(shell + 256.0 * mu)
    rolled = [pltpu.roll(t, 1, 0) for t in tiles[32:]]
    moved = [pltpu.roll(t, 32, 1) for t in rolled]
    for m in range(32):
        first = jnp.where(lane < 32, moved[m - 1], moved[m])
        tiles[32 + m] = jnp.where(sub == 0, first, rolled[m])
    for tile in range(64):
        top = jnp.floor(tiles[tile] * (1.0 / 128.0))
        at = ((tile % 32) * 2 + tile // 32) * 8
        high[at : at + 8, :] = top
        low[at : at + 8, :] = tiles[tile] - 128.0 * top

    for part in range(HALF // TK):
        rows = slice(part * TK, part * TK + TK)
        real[rows, :] = jnp.dot(cos_ref[rows, :], lines[...], preferred_element_type=jnp.float32)
        turn[rows, :] = jnp.dot(sin_ref[rows, :], lines[...], preferred_element_type=jnp.float32)

    spot = place[1]
    col = (lane & 31).astype(jnp.float32)
    wave_x = (NZ // 4 + spot // 2).astype(jnp.float32)
    wave_y = (NZ // 8 + (spot % 2) * 128 + place[0] * 32).astype(jnp.float32) + col
    plane_square = wave_x * wave_x + wave_y * wave_y
    weight_one = jnp.where(odd, wave_y * wave_y, wave_x * wave_x) * 1.5
    mixed = wave_x * wave_y * 3.0
    linear = jnp.where(odd, wave_y, wave_x) * 3.0
    turn_sign = jnp.where(upper, -1.0, 1.0)
    step16 = lax.broadcasted_iota(jnp.int32, (16, 128), 0).astype(jnp.float32).astype(jnp.bfloat16)
    step128 = lax.broadcasted_iota(jnp.int32, (128, 128), 0).astype(jnp.float32).astype(jnp.bfloat16)

    last_inverse = 1.0 / (plane_square + float(HALF) * HALF)
    for f in range(4):
        at = slice(f * 128, f * 128 + 128)
        a, b = real[0:8, at], pltpu.roll(turn[0:8, at], 64, 1) * turn_sign
        real[0:8, at] = jnp.where(sub == 0, 0.5 * (a - b), a)
        turn[0:8, at] = pltpu.roll(jnp.where(sub == 0, 0.5 * (a + b), b) * turn_sign, 64, 1)

    def tile_body(m, carry):
        products = [[], []]
        for q in range(4):
            at = pl.multiple_of(m * 32 + q * 8, 8)
            k_row = at + sub
            first = k_row == 0
            wave_z = k_row.astype(jnp.float32)
            plain_square = wave_z * wave_z
            plain_inverse = 1.0 / (plane_square + plain_square)
            for sign in range(2):
                kz = wave_z if sign == 0 else jnp.where(first, -float(HALF), -wave_z)
                square = plain_square if sign == 0 else jnp.where(first, float(HALF) * HALF, plain_square)
                inverse = plain_inverse if sign == 0 else jnp.where(first, last_inverse, plain_inverse)
                weights = (
                    None,
                    weight_one * inverse,
                    jnp.where(odd, mixed, 1.5 * square) * inverse,
                    linear * kz * inverse,
                )
                spectra = []
                for f in range(4):
                    a = real[pl.ds(at, 8), f * 128 : f * 128 + 128]
                    b = pltpu.roll(turn[pl.ds(at, 8), f * 128 : f * 128 + 128], 64, 1) * turn_sign
                    spectra.append(a + b if sign == 0 else a - b)
                base = jnp.where(odd, pltpu.roll(spectra[0], 32, 1), spectra[0])
                cross = [base * s for s in spectra]
                products[sign].append([cross[0]] + [cross[f] * weights[f] for f in (1, 2, 3)])
        for sign in range(2):
            quad = products[sign]
            pairs = [
                (fold((quad[0][f], quad[2][f]), lane, 64), fold((quad[1][f], quad[3][f]), lane, 64))
                for f in range(4)
            ]
            even, other = pairs[0]
            tiles = [
                jnp.where(odd, pltpu.roll(other, 32, 1), even),
                jnp.where(odd, other, pltpu.roll(even, 96, 1)),
            ] + [fold(pairs[f], lane, 32) for f in (1, 2, 3)]
            at = pl.multiple_of(m * 16 + sign * 8, 8)
            lows = low[pl.ds(at, 8), :]
            highs = high[pl.ds(at, 8), :]
            total = None
            for r0 in range(0, 8, 4):
                vals, hots = [], []
                for r in range(r0, r0 + 4):
                    spread = jnp.broadcast_to(highs[r : r + 1], (16, 128)).astype(jnp.bfloat16)
                    hit = spread == step16
                    items = [jnp.broadcast_to(tiles[v][r : r + 1], (16, 128)).astype(jnp.bfloat16) for v in range(5)]
                    vals.append(jnp.concatenate(
                        [jnp.where(hit, item, jnp.bfloat16(0)) for item in items]
                        + [jnp.where(hit, jnp.bfloat16(1), jnp.bfloat16(0))], axis=0))
                    spread = jnp.broadcast_to(lows[r : r + 1], (16, 128)).astype(jnp.bfloat16)
                    hots.append(jnp.where(jnp.concatenate([spread] * 8, axis=0) == step128, jnp.bfloat16(1), jnp.bfloat16(0)))
                part = lax.dot_general(
                    jnp.concatenate(vals, axis=1), jnp.concatenate(hots, axis=1),
                    (((1,), (1,)), ((), ())), preferred_element_type=jnp.float32)
                total = part if total is None else total + part
            acc[...] += total
        return carry

    lax.fori_loop(0, HALF // 32, tile_body, 0, unroll=UNROLL)

    out_ref[0:32, :] = acc[0:32, :]
    out_ref[32:48, :] = acc[32:48, :] + acc[48:64, :] + acc[64:80, :] - 0.5 * acc[16:32, :]
    out_ref[48:64, :] = acc[80:96, :]


def bins(place, received, cos_table, sin_table):
    return pl.pallas_call(
        bins_kernel,
        in_specs=[pl.BlockSpec(memory_space=pltpu.SMEM)] + [pl.BlockSpec(memory_space=pltpu.VMEM)] * 3,
        out_specs=pl.BlockSpec(memory_space=pltpu.VMEM),
        scratch_shapes=[
            pltpu.VMEM((NZ, 512), jnp.bfloat16),
            pltpu.VMEM((512, 128), jnp.float32),
            pltpu.VMEM((512, 128), jnp.float32),
            pltpu.VMEM((HALF, 512), jnp.float32),
            pltpu.VMEM((HALF, 512), jnp.float32),
            pltpu.VMEM((96, 128), jnp.float32),
        ],
        out_shape=jax.ShapeDtypeStruct((64, 128), jnp.float32),
        compiler_params=pltpu.CompilerParams(vmem_limit_bytes=40 * 1024 * 1024),
        name="bins",
    )(place, received, cos_table, sin_table)


def total_over_devices(value):
    for bits in (1, 3, 9, 33, 7, 25, 97):
        value = value + lax.ppermute(value, BOTH, [(i, i ^ bits) for i in range(128)])
    return value


def body(fields, shells, mubins):
    field, spot = lax.axis_index("field"), lax.axis_index("gz")
    cos_table, sin_table = dft_tables()
    place = jnp.stack([field, spot, jnp.where(spot >= 16, 3 - field, field)]).astype(jnp.int32)
    sent = pack(place, fields, shells, mubins)
    received = lax.all_to_all(sent, BOTH, split_axis=0, concat_axis=0, tiled=True)
    partial = bins(place, received, jnp.asarray(cos_table), jnp.asarray(sin_table))
    total = total_over_devices(partial).reshape(4, MUBINS, SHELLS)
    return total[:3] / jnp.maximum(total[3], 1.0)[None]


def solution(mesh):
    in_specs = (P("gz", None, "field", None, None), P("gz", None, None), P("gz", None, None))
    return jax.shard_map(body, mesh=mesh, in_specs=in_specs, out_specs=P(), check_vma=False)
```

```python
import math

import jax
import jax.numpy as jnp
import numpy as np
from jax import lax
from jax.experimental import pallas as pl
from jax.experimental.pallas import tpu as pltpu
from jax.sharding import PartitionSpec as P

NZ = 2048
HALF = NZ // 2
SHELLS = 256
MUBINS = 8
PLANES = 16
YROWS = 256
COLS = 32
ROWS = 72
TK = 256
UNROLL = 16
BOTH = ("field", "gz")


def dft_tables():
    index = np.arange(NZ, dtype=np.int64)
    product = (np.arange(HALF + 1, dtype=np.int64)[:, None] * index[None, :]) % NZ
    angle = (product.astype(np.float32) * np.float32(2.0 * math.pi / NZ)).astype(np.float64)
    factor = np.float32(1.0 / math.sqrt(NZ))
    cos_rows = (np.cos(angle).astype(np.float32) * factor).astype(jnp.bfloat16)
    sin_rows = (np.sin(angle).astype(np.float32) * factor).astype(jnp.bfloat16)
    sin_rows[0] = cos_rows[HALF]
    return cos_rows[:HALF], sin_rows[:HALF]


def swap_groups(parts, lane):
    upper = lane >= 64
    odd = (lane & 32) != 0
    a, b, c, d = parts
    a, c = jnp.where(upper, pltpu.roll(c, 64, 1), a), jnp.where(upper, c, pltpu.roll(a, 64, 1))
    b, d = jnp.where(upper, pltpu.roll(d, 64, 1), b), jnp.where(upper, d, pltpu.roll(b, 64, 1))
    a, b = jnp.where(odd, pltpu.roll(b, 32, 1), a), jnp.where(odd, b, pltpu.roll(a, 96, 1))
    c, d = jnp.where(odd, pltpu.roll(d, 32, 1), c), jnp.where(odd, d, pltpu.roll(c, 96, 1))
    return a, b, c, d


def pack_kernel(place, fields_hbm, shells_hbm, mubins_hbm, out_ref, fields_ref, index_ref, field_sems, index_sems):
    spot = pl.multiple_of(place[2] * 16, 16)
    copies = [
        pltpu.make_async_copy(
            fields_hbm.at[pl.ds(part * 16, 16)], fields_ref.at[pl.ds(part * 16, 16)], field_sems.at[part]
        )
        for part in range(4)
    ]
    index_copies = [
        pltpu.make_async_copy(source.at[pl.ds(spot, 16)], index_ref.at[n], index_sems.at[n])
        for n, source in enumerate((shells_hbm, mubins_hbm))
    ]
    for copy in index_copies + copies:
        copy.start()
    row = lax.broadcasted_iota(jnp.int32, (256, 256), 0)
    col = lax.broadcasted_iota(jnp.int32, (256, 256), 1)
    lane = lax.broadcasted_iota(jnp.int32, (256, 128), 1)
    inner = row % 16
    order = (col == inner * 16 + row // 16).astype(jnp.bfloat16)
    turned = jnp.where(place[1] >= 16, 15 - inner, inner)
    turned = (col == turned * 16 + row // 16).astype(jnp.bfloat16)

    for copy in index_copies + copies[:1]:
        copy.wait()
    maps = [
        jnp.dot(
            turned,
            index_ref[n].reshape(256, YROWS).astype(jnp.bfloat16),
            preferred_element_type=jnp.float32,
        ).reshape(16, 2, 8, YROWS)
        for n in range(2)
    ]
    groups = [item[:, h].reshape(128, YROWS) for item in maps for h in range(2)]
    for half in range(2):
        quarters = swap_groups([g[:, half * 128 : half * 128 + 128] for g in groups], lane[:128])
        for q in range(4):
            block = quarters[q].reshape(16, 8, 128)
            for p in range(PLANES):
                out_ref[q * 32 + p * 2 + half, 64:72, :] = block[p].astype(jnp.bfloat16)

    for part in range(4):
        if part == 1:
            for copy in copies[1:]:
                copy.wait()
        start = part * 16
        parts = [
            jnp.dot(
                order,
                fields_ref[start : start + 16, c, f].reshape(256, YROWS),
                preferred_element_type=jnp.float32,
            )
            for c in range(2)
            for f in range(2)
        ]
        for half in range(2):
            quarters = swap_groups([item[:, half * 128 : half * 128 + 128] for item in parts], lane)
            for q in range(4):
                block = quarters[q].astype(jnp.bfloat16).reshape(16, 16, 128)
                for p in range(PLANES):
                    out_ref[q * 32 + p * 2 + half, start : start + 16, :] = block[p]


def pack(place, fields, shells, mubins):
    return pl.pallas_call(
        pack_kernel,
        in_specs=[pl.BlockSpec(memory_space=pltpu.SMEM)] + [pl.BlockSpec(memory_space=pltpu.HBM)] * 3,
        out_specs=pl.BlockSpec(memory_space=pltpu.VMEM),
        scratch_shapes=[
            pltpu.VMEM((64, 2, 2, PLANES, YROWS), jnp.bfloat16),
            pltpu.VMEM((2, 16, PLANES, YROWS), jnp.int32),
            pltpu.SemaphoreType.DMA((4,)),
            pltpu.SemaphoreType.DMA((2,)),
        ],
        out_shape=jax.ShapeDtypeStruct((128, ROWS, 128), jnp.bfloat16),
        compiler_params=pltpu.CompilerParams(vmem_limit_bytes=32 * 1024 * 1024),
        name="pack",
    )(place, *[pltpu.with_memory_space_constraint(x, pltpu.HBM) for x in (fields, shells, mubins)])


def fold(parts, lane, width):
    first, second = parts
    odd = (lane & width) != 0
    kept = jnp.where(odd, second, first)
    moved = jnp.where(odd, first, second)
    return kept + pltpu.roll(moved, width, 1) if width == 64 else kept + swap32(moved, lane)


def swap32(value, lane):
    odd = (lane & 32) != 0
    return jnp.where(odd, pltpu.roll(value, 32, 1), pltpu.roll(value, 96, 1))


def bins_kernel(place, recv_ref, cos_ref, sin_ref, out_ref, lines, low, high, real, turn, acc):
    lane = lax.broadcasted_iota(jnp.int32, (8, 128), 1)
    sub = lax.broadcasted_iota(jnp.int32, (8, 128), 0)
    upper = lane >= 64
    odd = (lane & 32) != 0

    acc[...] = jnp.zeros_like(acc)
    for f in range(4):
        for j in range(32):
            lines[j * 64 : j * 64 + 64, f * 128 : f * 128 + 128] = recv_ref[f * 32 + j, 0:64, :]
    tiles = []
    for tile in range(64):
        turned = tile >= 32
        source = 31 - (tile - 32) // 2 if turned else tile // 2
        pair = (tile % 2) * 2
        one = recv_ref[pair * 32 + source, 64:72, :].astype(jnp.float32)
        two = recv_ref[(pair + 1) * 32 + source, 64:72, :].astype(jnp.float32)
        shell = jnp.where(upper, pltpu.roll(two, 64, 1), one)
        mu = jnp.where(upper, two, pltpu.roll(one, 64, 1))
        tiles.append(shell + 256.0 * mu)
    rolled = [pltpu.roll(t, 1, 0) for t in tiles[32:]]
    moved = [pltpu.roll(t, 32, 1) for t in rolled]
    for m in range(32):
        first = jnp.where(lane < 32, moved[m - 1], moved[m])
        tiles[32 + m] = jnp.where(sub == 0, first, rolled[m])
    for tile in range(64):
        top = jnp.floor(tiles[tile] * (1.0 / 128.0))
        at = ((tile % 32) * 2 + tile // 32) * 8
        high[at : at + 8, :] = top
        low[at : at + 8, :] = tiles[tile] - 128.0 * top

    for part in range(HALF // TK):
        rows = slice(part * TK, part * TK + TK)
        real[rows, :] = jnp.dot(cos_ref[rows, :], lines[...], preferred_element_type=jnp.float32)
        turn[rows, :] = jnp.dot(sin_ref[rows, :], lines[...], preferred_element_type=jnp.float32)

    spot = place[1]
    col = (lane & 31).astype(jnp.float32)
    wave_x = (NZ // 4 + spot // 2).astype(jnp.float32)
    wave_y = (NZ // 8 + (spot % 2) * 128 + place[0] * 32).astype(jnp.float32) + col
    plane_square = wave_x * wave_x + wave_y * wave_y
    weight_one = jnp.where(odd, wave_y * wave_y, wave_x * wave_x) * 1.5
    mixed = wave_x * wave_y * 3.0
    linear = jnp.where(odd, wave_y, wave_x) * 3.0
    turn_sign = jnp.where(upper, -1.0, 1.0)
    step16 = lax.broadcasted_iota(jnp.int32, (16, 128), 0).astype(jnp.float32).astype(jnp.bfloat16)
    step128 = lax.broadcasted_iota(jnp.int32, (128, 128), 0).astype(jnp.float32).astype(jnp.bfloat16)

    last_inverse = 1.0 / (plane_square + float(HALF) * HALF)
    for f in range(4):
        at = slice(f * 128, f * 128 + 128)
        a, b = real[0:8, at], pltpu.roll(turn[0:8, at], 64, 1) * turn_sign
        real[0:8, at] = jnp.where(sub == 0, 0.5 * (a - b), a)
        turn[0:8, at] = pltpu.roll(jnp.where(sub == 0, 0.5 * (a + b), b) * turn_sign, 64, 1)

    def tile_body(m, carry):
        products = [[], []]
        for q in range(4):
            at = pl.multiple_of(m * 32 + q * 8, 8)
            k_row = at + sub
            first = k_row == 0
            wave_z = k_row.astype(jnp.float32)
            plain_square = wave_z * wave_z
            plain_inverse = 1.0 / (plane_square + plain_square)
            for sign in range(2):
                kz = wave_z if sign == 0 else jnp.where(first, -float(HALF), -wave_z)
                square = plain_square if sign == 0 else jnp.where(first, float(HALF) * HALF, plain_square)
                inverse = plain_inverse if sign == 0 else jnp.where(first, last_inverse, plain_inverse)
                weights = (
                    None,
                    weight_one * inverse,
                    jnp.where(odd, mixed, 1.5 * square) * inverse,
                    linear * kz * inverse,
                )
                spectra = []
                for f in range(4):
                    a = real[pl.ds(at, 8), f * 128 : f * 128 + 128]
                    b = pltpu.roll(turn[pl.ds(at, 8), f * 128 : f * 128 + 128], 64, 1) * turn_sign
                    spectra.append(a + b if sign == 0 else a - b)
                base = jnp.where(odd, pltpu.roll(spectra[0], 32, 1), spectra[0])
                cross = [base * s for s in spectra]
                products[sign].append([cross[0]] + [cross[f] * weights[f] for f in (1, 2, 3)])
        for sign in range(2):
            quad = products[sign]
            pairs = [
                (fold((quad[0][f], quad[2][f]), lane, 64), fold((quad[1][f], quad[3][f]), lane, 64))
                for f in range(4)
            ]
            even, other = pairs[0]
            tiles = [
                jnp.where(odd, pltpu.roll(other, 32, 1), even),
                jnp.where(odd, other, pltpu.roll(even, 96, 1)),
            ] + [fold(pairs[f], lane, 32) for f in (1, 2, 3)]
            at = pl.multiple_of(m * 16 + sign * 8, 8)
            lows = low[pl.ds(at, 8), :]
            highs = high[pl.ds(at, 8), :]
            total = None
            for r0 in range(0, 8, 4):
                vals, hots = [], []
                for r in range(r0, r0 + 4):
                    spread = jnp.broadcast_to(highs[r : r + 1], (16, 128)).astype(jnp.bfloat16)
                    hit = spread == step16
                    items = [jnp.broadcast_to(tiles[v][r : r + 1], (16, 128)).astype(jnp.bfloat16) for v in range(5)]
                    vals.append(jnp.concatenate(
                        [jnp.where(hit, item, jnp.bfloat16(0)) for item in items]
                        + [jnp.where(hit, jnp.bfloat16(1), jnp.bfloat16(0))], axis=0))
                    spread = jnp.broadcast_to(lows[r : r + 1], (16, 128)).astype(jnp.bfloat16)
                    hots.append(jnp.where(jnp.concatenate([spread] * 8, axis=0) == step128, jnp.bfloat16(1), jnp.bfloat16(0)))
                part = lax.dot_general(
                    jnp.concatenate(vals, axis=1), jnp.concatenate(hots, axis=1),
                    (((1,), (1,)), ((), ())), preferred_element_type=jnp.float32)
                total = part if total is None else total + part
            acc[...] += total
        return carry

    lax.fori_loop(0, HALF // 32, tile_body, 0, unroll=UNROLL)

    out_ref[0:32, :] = acc[0:32, :]
    out_ref[32:48, :] = acc[32:48, :] + acc[48:64, :] + acc[64:80, :] - 0.5 * acc[16:32, :]
    out_ref[48:64, :] = acc[80:96, :]


def bins(place, received, cos_table, sin_table):
    return pl.pallas_call(
        bins_kernel,
        in_specs=[pl.BlockSpec(memory_space=pltpu.SMEM)] + [pl.BlockSpec(memory_space=pltpu.VMEM)] * 3,
        out_specs=pl.BlockSpec(memory_space=pltpu.VMEM),
        scratch_shapes=[
            pltpu.VMEM((NZ, 512), jnp.bfloat16),
            pltpu.VMEM((512, 128), jnp.float32),
            pltpu.VMEM((512, 128), jnp.float32),
            pltpu.VMEM((HALF, 512), jnp.float32),
            pltpu.VMEM((HALF, 512), jnp.float32),
            pltpu.VMEM((96, 128), jnp.float32),
        ],
        out_shape=jax.ShapeDtypeStruct((64, 128), jnp.float32),
        compiler_params=pltpu.CompilerParams(vmem_limit_bytes=40 * 1024 * 1024),
        name="bins",
    )(place, received, cos_table, sin_table)


def total_over_devices(value):
    for bits in (1, 3, 9, 33, 7, 25, 97):
        value = value + lax.ppermute(value, BOTH, [(i, i ^ bits) for i in range(128)])
    return value


def body(fields, shells, mubins):
    field, spot = lax.axis_index("field"), lax.axis_index("gz")
    cos_table, sin_table = dft_tables()
    place = jnp.stack([field, spot, jnp.where(spot >= 16, 3 - field, field)]).astype(jnp.int32)
    sent = pack(place, fields, shells, mubins)
    received = lax.all_to_all(sent, BOTH, split_axis=0, concat_axis=0, tiled=True)
    partial = bins(place, received, jnp.asarray(cos_table), jnp.asarray(sin_table))
    total = total_over_devices(partial).reshape(4, MUBINS, SHELLS)
    return total[:3] / jnp.maximum(total[3], 1.0)[None]


def solution(mesh):
    in_specs = (P("gz", None, "field", None, None), P("gz", None, None), P("gz", None, None))
    return jax.shard_map(body, mesh=mesh, in_specs=in_specs, out_specs=P(), check_vma=False)
```
